32 devices in a mesh: grp: 8 (over y, x, core), sh: 4 (over z).
Axes of the slice: x: 2, y: 2, z: 4, core: 2. Of those that a mesh axis runs over, the one named last changes fastest.
Arguments:
- factors: bfloat16 [24, 128, 14336], P('grp', None, 'sh'), may hold values from -0.5 to 0.5
- screen: int32 [24, 1, 112], P('grp', None, 'sh'), may hold values 0 or 1
- occ_energy: float32 [24], replicated, may hold values from -1.5 to -0.3
- virt_energy: float32 [128], replicated, may hold values from 0.5 to 3
Outputs:
- gamma: bfloat16 [24, 128, 14336], P('grp', 'sh')
The draws below stay inside these ranges and needn't reach their ends.
Inputs may be any that keep to these rules, and one draw needn't show every extreme that they name: `screen`: 1 keeps a block of 128 virtual by 128 auxiliary functions of one occupied orbital, 0 screens it out.
All inputs are finite; a program needn't handle non-finite values.
Results may differ from the reference program's by a relative error of at most 0.0049.
Values may be sent and summed in bfloat16 or wider, within the bound.
A program may use at most 64 MiB of HBM per device.

```python
import jax
import jax.numpy as jnp
from jax import lax

VIRT = 128
BLK = 128
NAUX = 14336
OCC = 24


def plant(entries, rng, low, top_value):
    spot = [jax.random.randint(jax.random.fold_in(rng, axis), (), 0, length) for axis, length in enumerate(entries.shape)]
    main_axis = entries.shape.index(max(entries.shape))
    neighbour = spot[:main_axis] + [(spot[main_axis] + 1) % entries.shape[main_axis]] + spot[main_axis + 1:]
    return entries.at[tuple(spot)].set(low).at[tuple(neighbour)].set(top_value)


def shard_levels(own_key, dims, pieces, smallest, top_value):
    def one(axis_at, blocks):
        draws = jax.random.uniform(jax.random.fold_in(jax.random.fold_in(own_key, 6), axis_at), (blocks,), jnp.float32, smallest / len(pieces), top_value / len(pieces))
        return jnp.repeat(jnp.exp(draws), dims[axis_at] // blocks).reshape((-1,) + (1,) * (len(dims) - axis_at - 1))

    factor_of = one(*pieces[0])
    for cut in pieces[1:]:
        factor_of = factor_of * one(*cut)
    return factor_of


def centred(own_key, extent, deviation, most, cuts=(), dtype=jnp.bfloat16):
    factor_of = shard_levels(own_key, extent, cuts, -0.22, 0.18) if cuts else 1.0
    drawn = jax.random.normal(own_key, extent, jnp.float32) * deviation * factor_of
    return jnp.minimum(jnp.maximum(drawn, -most), most).astype(dtype)


def setup_inputs(seed: int = 0) -> dict:
    keys = jax.random.split(jax.random.key(seed), 5)
    factors = centred(keys[0], (OCC, VIRT, NAUX), 0.09, 0.5, ((0, 8), (2, 4)))
    screen = plant((jax.random.randint(keys[1], (OCC, VIRT // BLK, NAUX // BLK), 0, 4) < 3).astype(jnp.int32), jax.random.fold_in(keys[1], 1), 0, 1)
    occ_energy = jnp.clip(jax.random.uniform(keys[2], (OCC,), jnp.float32, -1.5, -0.3), -1.5, -0.3)
    virt_energy = jnp.clip(jax.random.uniform(keys[3], (VIRT,), jnp.float32, 0.5, 3.0), 0.5, 3.0)
    return {"factors": factors, "screen": screen, "occ_energy": occ_energy, "virt_energy": virt_energy}


def reference(factors, screen, occ_energy, virt_energy):
    occ_all, virt_width, aux_width = factors.shape
    wide_mask = jnp.repeat(jnp.repeat(screen, BLK, axis=1), BLK, axis=2)
    screened = (factors * wide_mask.astype(jnp.bfloat16)).reshape(occ_all * virt_width, aux_width)
    coulomb = lax.dot_general(screened, screened, (((1,), (1,)), ((), ())), preferred_element_type=jnp.float32)
    row_energy = (virt_energy[None, :] - occ_energy[:, None]).reshape(-1)
    amplitude = (coulomb / (row_energy[:, None] + row_energy[None, :])).astype(jnp.bfloat16)
    four_index = amplitude.reshape(occ_all, virt_width, occ_all, virt_width).astype(jnp.float32)
    combined = (2.0 * four_index - jnp.transpose(four_index, (0, 3, 2, 1))).astype(jnp.bfloat16)
    combined = combined.reshape(occ_all * virt_width, occ_all * virt_width)
    gamma = jnp.dot(combined, screened, preferred_element_type=jnp.float32).astype(jnp.bfloat16)
    return gamma.reshape(occ_all, virt_width, aux_width)
```

```python
import functools

import jax
import jax.numpy as jnp
from jax import lax
from jax.experimental import pallas as pl
from jax.experimental.pallas import tpu as pltpu
from jax.sharding import PartitionSpec as P

BLK = 128
MESH = pl.DeviceIdType.MESH


def amplitude_kernel(
    dims, own_hbm, own_energy, all_energy, out, blocks, own_t, part32, part16, arrived, amp, tile32, weight, staged,
    own_sem, ring_send, ring_recv, twin_send, twin_recv, part_send, part_recv, amp_send, amp_recv, out_send, out_recv,
    out_local,
):
    occ_g, virt, aux, groups, shards = dims
    rows = occ_g * virt
    piece = rows // 2
    share = piece // shards
    slab = virt // shards
    chips = groups // 2
    span = chips // 2
    me_g, me_z = lax.axis_index("grp"), lax.axis_index("sh")
    core = lax.rem(me_g, 2)
    chip = lax.div(me_g, 2)
    odd, line = lax.rem(chip, 2), lax.div(chip, 2)
    spot = line + odd * (chips - 1 - 2 * line)

    def at(offset, other):
        place = lax.rem(spot + offset + chips, chips)
        that = 2 * place + lax.div(place, span) * (2 * chips - 1 - 4 * place)
        return 2 * that + (1 - core if other else core)

    def rows_of(offset, other, half):
        return pl.ds(pl.multiple_of((2 * at(offset, other) + half) * piece, piece), piece)

    right, left, twin = at(1, False), at(-1, False), at(0, True)
    peers = [lax.rem(me_z + q, shards) for q in range(1, shards)]
    before = [lax.rem(me_z - q + shards, shards) for q in range(1, shards)]

    load = pltpu.make_async_copy(own_hbm, blocks.at[pl.ds(pl.multiple_of(me_g * rows, rows), rows)], own_sem)
    load.start()
    barrier = pltpu.get_barrier_semaphore()
    for g in (right, left, twin):
        pl.semaphore_signal(barrier, inc=1, device_id=(g, me_z), device_id_type=MESH)
    for z in peers:
        pl.semaphore_signal(barrier, inc=1, device_id=(me_g, z), device_id_type=MESH)
    pl.semaphore_wait(barrier, 3 + shards - 1)
    load.wait()

    sent = []

    def ring(way, step, half):
        back = -(step - 1) if way == 0 else step - 1
        where = rows_of(back, False, half)
        return pltpu.make_async_remote_copy(
            src_ref=blocks.at[where], dst_ref=blocks.at[where],
            send_sem=ring_send.at[way, step - 1, half], recv_sem=ring_recv.at[way, step - 1, half],
            device_id=(right if way == 0 else left, me_z), device_id_type=MESH,
        )

    def ring_in(way, step, half):
        where = rows_of(-step if way == 0 else step, False, half)
        return pltpu.make_async_remote_copy(
            src_ref=blocks.at[where], dst_ref=blocks.at[where],
            send_sem=ring_send.at[way, step - 1, half], recv_sem=ring_recv.at[way, step - 1, half],
            device_id=(right if way == 0 else left, me_z), device_id_type=MESH,
        )

    def to_twin(offset, other, half, index):
        where = rows_of(offset, other, half)
        return pltpu.make_async_remote_copy(
            src_ref=blocks.at[where], dst_ref=blocks.at[where],
            send_sem=twin_send.at[index], recv_sem=twin_recv.at[index],
            device_id=(twin, me_z), device_id_type=MESH,
        )

    def go(copy):
        copy.start()
        sent.append(copy)

    halves = lambda way, step: ((0, 1) if way == 0 else (1, 0)) if step < span else ((0,) if way == 0 else (1,))

    for turn in range(2):
        for way in (0, 1):
            if turn < len(halves(way, 1)):
                go(ring(way, 1, halves(way, 1)[turn]))
    for half in (0, 1):
        go(to_twin(0, False, half, half))

    depth = BLK * 4 if aux % (BLK * 4) == 0 else BLK
    own_rows = pl.ds(pl.multiple_of(me_g * rows, rows), rows)

    @pl.loop(0, aux // depth)
    def _(k):
        at_k = pl.ds(pl.multiple_of(k * depth, depth), depth)
        own_t[at_k, :] = blocks[own_rows, at_k].astype(jnp.float32).T.astype(jnp.bfloat16)

    batches = [[(0, 0, None, 0, 0), (0, 1, None, 0, 1)]]
    index = 2
    for step in range(1, span + 1):
        for turn in range(len(halves(0, step))):
            batch = []
            for way in (0, 1):
                half = halves(way, step)[turn]
                batch.append((-step if way == 0 else step, half, way, step, index))
                index += 1
            batches.append(batch)

    def product(where, index):
        part32[...] = jnp.zeros_like(part32)

        @pl.loop(0, aux // depth)
        def _(k):
            at_k = pl.ds(pl.multiple_of(k * depth, depth), depth)
            part32[...] += jnp.dot(blocks[where, at_k], own_t[at_k, :], preferred_element_type=jnp.float32)

        for q in range(shards):
            part16[index, q] = part32[q * share:(q + 1) * share, :].astype(jnp.bfloat16)
        for q, z in enumerate(peers):
            go(pltpu.make_async_remote_copy(
                src_ref=part16.at[index, z], dst_ref=arrived.at[index, q],
                send_sem=part_send.at[index, q], recv_sem=part_recv.at[index, q],
                device_id=(me_g, z), device_id_type=MESH,
            ))

    def divide(offset, other, half, index):
        total = part16[index, me_z].astype(jnp.float32)
        for q in range(shards - 1):
            pltpu.make_async_copy(arrived.at[index, q], arrived.at[index, q], part_recv.at[index, q]).wait()
            total += arrived[index, q].astype(jnp.float32)
        gap = all_energy[2 * at(offset, other) + half, me_z] + own_energy[...]
        amp[index, me_z] = (total / gap).astype(jnp.bfloat16)
        for q, z in enumerate(peers):
            go(pltpu.make_async_remote_copy(
                src_ref=amp.at[index, me_z], dst_ref=amp.at[index, me_z],
                send_sem=amp_send.at[index, q], recv_sem=amp_recv.at[index, q],
                device_id=(me_g, z), device_id_type=MESH,
            ))

    def combine(offset, other, indices):
        for half in (0, 1):
            for q, z in enumerate(before):
                slot = amp.at[indices[half], z]
                pltpu.make_async_copy(slot, slot, amp_recv.at[indices[half], q]).wait()
            for q in range(shards):
                low = half * piece + q * share
                tile32[low:low + share, :] = amp[indices[half], q].astype(jnp.float32)
        first = at(offset, other) * rows
        for j in range(occ_g):
            columns = pl.ds(pl.multiple_of(first + j * virt, virt), virt)
            for i in range(occ_g):
                tile = tile32[j * virt:(j + 1) * virt, i * virt:(i + 1) * virt]
                weight[i * virt:(i + 1) * virt, columns] = (2.0 * tile.T - tile).astype(jnp.bfloat16)

    seen = {}
    ready = []
    for batch in batches:
        work = []
        for offset, half, way, step, index in batch:
            if way is not None:
                ring_in(way, step, half).wait_recv()
                if step < span and half in halves(way, step + 1):
                    go(ring(way, step + 1, half))
                go(to_twin(offset, False, half, index))
            work.append((offset, False, half, 2 * index))
        for offset, other, half, index in work:
            product(rows_of(offset, other, half), index)
        for offset, half, way, step, index in batch:
            to_twin(offset, True, half, index).wait_recv()
            product(rows_of(offset, True, half), 2 * index + 1)
            work.append((offset, True, half, 2 * index + 1))
        for entry in work:
            divide(*entry)
        for entry in ready:
            combine(*entry)
        ready = []
        for offset, other, half, index in work:
            key = (offset % chips, other)
            seen.setdefault(key, {})[half] = index
            if len(seen[key]) == 2:
                ready.append((offset, other, seen[key]))
    for entry in ready:
        combine(*entry)

    wide = depth
    turns = aux // wide

    def out_copy(c, q, z, source):
        return pltpu.make_async_remote_copy(
            src_ref=staged.at[z, :, :, pl.ds(pl.multiple_of(c * wide, wide), wide)],
            dst_ref=out.at[:, :, pl.ds(pl.multiple_of(source * aux + c * wide, wide), wide)],
            send_sem=out_send.at[c, q], recv_sem=out_recv.at[c, q],
            device_id=(me_g, z), device_id_type=MESH,
        )

    def out_own(c):
        return pltpu.make_async_copy(
            staged.at[me_z, :, :, pl.ds(pl.multiple_of(c * wide, wide), wide)],
            out.at[:, :, pl.ds(pl.multiple_of(me_z * aux + c * wide, wide), wide)],
            out_local.at[c],
        )

    @pl.loop(0, turns)
    def _(c):
        here = pl.ds(pl.multiple_of(c * wide, wide), wide)
        gamma = jnp.dot(weight[...], blocks[:, here], preferred_element_type=jnp.float32)
        for i in range(occ_g):
            for q in range(shards):
                low = i * virt + q * slab
                staged[q, i, :, here] = gamma[low:low + slab, :].astype(jnp.bfloat16)
        for q, z in enumerate(peers):
            out_copy(c, q, z, me_z).start()
        out_own(c).start()

    for copy in sent:
        copy.wait_send()

    @pl.loop(0, turns)
    def _(c):
        for q, z in enumerate(peers):
            out_copy(c, q, z, me_z).wait_send()
            out_copy(c, q, z, before[q]).wait_recv()
        out_own(c).wait()


def on_device(factors, screen, occ_energy, virt_energy):
    occ_g, virt, aux = factors.shape
    groups, shards = lax.axis_size("grp"), lax.axis_size("sh")
    rows = occ_g * virt
    piece = rows // 2
    share = piece // shards
    slab = virt // shards
    chips = groups // 2
    span = chips // 2
    pieces = 2 * groups
    wide = BLK * 4 if aux % (BLK * 4) == 0 else BLK
    turns = aux // wide
    wide_mask = jnp.repeat(jnp.repeat(screen, BLK, axis=1), BLK, axis=2)
    own_block = (factors * wide_mask.astype(jnp.bfloat16)).reshape(rows, aux)
    energy = virt_energy[None, :] - occ_energy[:, None]
    occ_own = lax.dynamic_slice_in_dim(occ_energy, lax.axis_index("grp") * occ_g, occ_g)
    own_energy = (virt_energy[None, :] - occ_own[:, None]).reshape(1, rows)
    all_energy = energy.reshape(pieces, shards, share, 1)
    dma = pltpu.SemaphoreType.DMA
    bf16 = jnp.bfloat16
    vmem = pl.BlockSpec(memory_space=pltpu.VMEM)
    return pl.pallas_call(
        functools.partial(amplitude_kernel, (occ_g, virt, aux, groups, shards)),
        out_shape=jax.ShapeDtypeStruct((occ_g, slab, aux * shards), bf16),
        in_specs=[pl.BlockSpec(memory_space=pl.ANY), vmem, vmem],
        out_specs=pl.BlockSpec(memory_space=pl.ANY),
        scratch_shapes=[
            pltpu.VMEM((groups * rows, aux), bf16),
            pltpu.VMEM((aux, rows), bf16),
            pltpu.VMEM((piece, rows), jnp.float32),
            pltpu.VMEM((pieces, shards, share, rows), bf16),
            pltpu.VMEM((pieces, shards - 1, share, rows), bf16),
            pltpu.VMEM((pieces, shards, share, rows), bf16),
            pltpu.VMEM((rows, rows), jnp.float32),
            pltpu.VMEM((rows, groups * rows), bf16),
            pltpu.VMEM((shards, occ_g, slab, aux), bf16),
            dma,
            dma((2, span, 2)),
            dma((2, span, 2)),
            dma((groups,)),
            dma((groups,)),
            dma((pieces, shards - 1)),
            dma((pieces, shards - 1)),
            dma((pieces, shards - 1)),
            dma((pieces, shards - 1)),
            dma((turns, shards - 1)),
            dma((turns, shards - 1)),
            dma((turns,)),
        ],
        cost_estimate=pl.CostEstimate(
            flops=4 * rows * groups * rows * aux, bytes_accessed=4 * rows * aux, transcendentals=0
        ),
        compiler_params=pltpu.CompilerParams(
            collective_id=0, has_side_effects=True, vmem_limit_bytes=56 * 1024 * 1024
        ),
    )(own_block, own_energy, all_energy)


def solution(mesh):
    placed = (P("grp", None, "sh"), P("grp", None, "sh"), P(), P())
    return jax.shard_map(
        on_device, mesh=mesh, in_specs=placed, out_specs=P("grp", "sh", None), check_vma=False
    )
```

```python
import functools

import jax
import jax.numpy as jnp
from jax import lax
from jax.experimental import pallas as pl
from jax.experimental.pallas import tpu as pltpu
from jax.sharding import PartitionSpec as P

BLK = 128
PIECE = 64
WINDOW = 2
MESH = pl.DeviceIdType.MESH


def amplitude_kernel(
    dims, own_hbm, screen, occ_energy, virt_energy, out, blocks, own_t, part32, part16, arrived, amp, tile32, turned,
    energy, weight, staged, own_sem, ring_send, ring_recv, twin_send, twin_recv, part_send, part_recv, amp_send,
    amp_recv, out_send, out_recv, out_local,
):
    occ_g, virt, aux, groups, shards = dims
    rows = occ_g * virt
    per_block = rows // PIECE
    per_orbital = virt // PIECE
    share = PIECE // shards
    slab = virt // shards
    chips = groups // 2
    span = chips // 2
    rounds = per_block * (span - 1) + per_block // 2
    me_g, me_z = lax.axis_index("grp"), lax.axis_index("sh")
    core = lax.rem(me_g, 2)
    chip = lax.div(me_g, 2)
    odd, line = lax.rem(chip, 2), lax.div(chip, 2)
    spot = line + odd * (chips - 1 - 2 * line)

    def at(offset, other):
        place = lax.rem(spot + offset + chips, chips)
        that = 2 * place + lax.div(place, span) * (2 * chips - 1 - 4 * place)
        return 2 * that + (1 - core if other else core)

    def rows_of(offset, other, chunk):
        return pl.ds(pl.multiple_of((per_block * at(offset, other) + chunk) * PIECE, PIECE), PIECE)

    right, left, twin = at(1, False), at(-1, False), at(0, True)
    peers = [lax.rem(me_z + q, shards) for q in range(1, shards)]
    before = [lax.rem(me_z - q + shards, shards) for q in range(1, shards)]

    own_rows = pl.ds(pl.multiple_of(me_g * rows, rows), rows)
    load = pltpu.make_async_copy(own_hbm, blocks.at[own_rows], own_sem)
    load.start()
    barrier = pltpu.get_barrier_semaphore()
    for g in (right, left, twin):
        pl.semaphore_signal(barrier, inc=1, device_id=(g, me_z), device_id_type=MESH)
    for z in peers:
        pl.semaphore_signal(barrier, inc=1, device_id=(me_g, z), device_id_type=MESH)
    load.wait()

    @pl.loop(0, aux // BLK)
    def _(p):
        columns = pl.ds(pl.multiple_of(p * BLK, BLK), BLK)
        for i in range(occ_g):
            keep = screen[i, 0, p].astype(jnp.float32)
            here = pl.ds(pl.multiple_of(me_g * rows + i * virt, virt), virt)
            blocks[here, columns] = (blocks[here, columns].astype(jnp.float32) * keep).astype(jnp.bfloat16)

    pl.semaphore_wait(barrier, 3 + shards - 1)

    sent = []

    def started(copy):
        copy.start()
        return copy

    def go(copy):
        sent.append(started(copy))

    def place_of(way, turn):
        step, rank = turn // per_block + 1, turn % per_block
        return step, (rank if way == 0 else per_block - 1 - rank)

    def ring(way, turn, receiving):
        step, chunk = place_of(way, turn)
        back = step if receiving else step - 1
        where = rows_of(-back if way == 0 else back, False, chunk)
        return pltpu.make_async_remote_copy(
            src_ref=blocks.at[where], dst_ref=blocks.at[where],
            send_sem=ring_send.at[way, turn], recv_sem=ring_recv.at[way, turn],
            device_id=(right if way == 0 else left, me_z), device_id_type=MESH,
        )

    def to_twin(offset, other, chunk, index):
        where = rows_of(offset, other, chunk)
        return pltpu.make_async_remote_copy(
            src_ref=blocks.at[where], dst_ref=blocks.at[where],
            send_sem=twin_send.at[index], recv_sem=twin_recv.at[index],
            device_id=(twin, me_z), device_id_type=MESH,
        )

    flying = {}
    for turn in range(min(WINDOW, rounds)):
        flying[turn] = [started(ring(way, turn, False)) for way in (0, 1)]
    for chunk in range(per_block):
        go(to_twin(0, False, chunk, chunk))

    depth = BLK * 4 if aux % (BLK * 4) == 0 else BLK

    @pl.loop(0, aux // depth)
    def _(k):
        at_k = pl.ds(pl.multiple_of(k * depth, depth), depth)
        own_t[at_k, :] = blocks[own_rows, at_k].astype(jnp.float32).T.astype(jnp.bfloat16)

    turned[...] = jnp.broadcast_to(virt_energy[...], (virt, virt)).T

    @pl.loop(0, groups * occ_g)
    def _(j):
        for part in range(per_orbital):
            for q in range(shards):
                low = part * PIECE + q * share
                energy[j * per_orbital + part, q] = turned[low:low + share, :] - occ_energy[j]

    own_energy = jnp.concatenate([virt_energy[...] - occ_energy[me_g * occ_g + i] for i in range(occ_g)], axis=1)

    def product(batch, number):
        part32[...] = jnp.zeros_like(part32)

        @pl.loop(0, aux // depth)
        def _(k):
            at_k = pl.ds(pl.multiple_of(k * depth, depth), depth)
            left_side = jnp.concatenate([blocks[rows_of(*entry), at_k] for entry in batch], axis=0)
            part32[...] += jnp.dot(left_side, own_t[at_k, :], preferred_element_type=jnp.float32)

        for c in range(len(batch)):
            for q in range(shards):
                low = c * PIECE + q * share
                part16[number, q, c] = part32[low:low + share, :].astype(jnp.bfloat16)
        for q, z in enumerate(peers):
            go(pltpu.make_async_remote_copy(
                src_ref=part16.at[number, z], dst_ref=arrived.at[number, q],
                send_sem=part_send.at[number, q], recv_sem=part_recv.at[number, q],
                device_id=(me_g, z), device_id_type=MESH,
            ))

    def divide(batch, number):
        for q in range(shards - 1):
            pltpu.make_async_copy(arrived.at[number, q], arrived.at[number, q], part_recv.at[number, q]).wait()
        for c, (offset, other, chunk) in enumerate(batch):
            total = part16[number, me_z, c].astype(jnp.float32)
            for q in range(shards - 1):
                total += arrived[number, q, c].astype(jnp.float32)
            theirs = energy[per_block * at(offset, other) + chunk, me_z]
            gap = jnp.concatenate([theirs] * occ_g, axis=1) + own_energy
            amp[number, me_z, c] = (total / gap).astype(jnp.bfloat16)
        for q, z in enumerate(peers):
            go(pltpu.make_async_remote_copy(
                src_ref=amp.at[number, me_z], dst_ref=amp.at[number, me_z],
                send_sem=amp_send.at[number, q], recv_sem=amp_recv.at[number, q],
                device_id=(me_g, z), device_id_type=MESH,
            ))

    seen = {}

    def combine(batch, number):
        for q, z in enumerate(before):
            slot = amp.at[number, z]
            pltpu.make_async_copy(slot, slot, amp_recv.at[number, q]).wait()
        for c, (offset, other, chunk) in enumerate(batch):
            j = chunk // per_orbital
            key = (offset % chips, other, j)
            seen.setdefault(key, {})[chunk % per_orbital] = (number, c)
            if len(seen[key]) < per_orbital:
                continue
            for part, (n, at_c) in seen[key].items():
                for q in range(shards):
                    low = part * PIECE + q * share
                    tile32[low:low + share, :] = amp[n, q, at_c].astype(jnp.float32)
            columns = pl.ds(pl.multiple_of(at(offset, other) * rows + j * virt, virt), virt)
            for i in range(occ_g):
                tile = tile32[:, i * virt:(i + 1) * virt]
                weight[i * virt:(i + 1) * virt, columns] = (2.0 * tile.T - tile).astype(jnp.bfloat16)

    home = [(0, False, c) for c in range(per_block)] + [(0, True, c) for c in range(per_block)]
    batches = [home[b:b + 4] for b in range(0, len(home), 4)]
    first = len(batches)
    for number, batch in enumerate(batches):
        for offset, other, chunk in batch:
            if other:
                to_twin(0, True, chunk, chunk).wait_recv()
        product(batch, number)
        if number >= 1:
            divide(batches[number - 1], number - 1)
        if number >= 2:
            combine(batches[number - 2], number - 2)
    for turn in range(rounds):
        number = first + turn
        batch = []
        for way in (0, 1):
            step, chunk = place_of(way, turn)
            batch.append((-step if way == 0 else step, False, chunk))
        for way in (0, 1):
            ring(way, turn, True).wait_recv()
            go(to_twin(*batch[way], per_block + 2 * turn + way))
        for copy in flying[turn]:
            copy.wait_send()
        if turn + WINDOW < rounds:
            flying[turn + WINDOW] = [started(ring(way, turn + WINDOW, False)) for way in (0, 1)]
        divide(batches[number - 1], number - 1)
        for way in (0, 1):
            offset, _, chunk = batch[way]
            to_twin(offset, True, chunk, per_block + 2 * turn + way).wait_recv()
        batch = batch + [(offset, True, chunk) for offset, _, chunk in batch]
        batches.append(batch)
        product(batch, number)
        if number >= 2:
            combine(batches[number - 2], number - 2)
    last = len(batches) - 1
    divide(batches[last], last)
    combine(batches[last - 1], last - 1)
    combine(batches[last], last)

    wide = depth
    turns = aux // wide

    def out_copy(c, q, z, source):
        return pltpu.make_async_remote_copy(
            src_ref=staged.at[z, :, :, pl.ds(pl.multiple_of(c * wide, wide), wide)],
            dst_ref=out.at[:, :, pl.ds(pl.multiple_of(source * aux + c * wide, wide), wide)],
            send_sem=out_send.at[c, q], recv_sem=out_recv.at[c, q],
            device_id=(me_g, z), device_id_type=MESH,
        )

    def out_own(c):
        return pltpu.make_async_copy(
            staged.at[me_z, :, :, pl.ds(pl.multiple_of(c * wide, wide), wide)],
            out.at[:, :, pl.ds(pl.multiple_of(me_z * aux + c * wide, wide), wide)],
            out_local.at[c],
        )

    @pl.loop(0, turns)
    def _(c):
        here = pl.ds(pl.multiple_of(c * wide, wide), wide)
        gamma = jnp.dot(weight[...], blocks[:, here], preferred_element_type=jnp.float32)
        for i in range(occ_g):
            for q in range(shards):
                low = i * virt + q * slab
                staged[q, i, :, here] = gamma[low:low + slab, :].astype(jnp.bfloat16)
        for q, z in enumerate(peers):
            out_copy(c, q, z, me_z).start()
        out_own(c).start()

    for copy in sent:
        copy.wait_send()

    @pl.loop(0, turns)
    def _(c):
        for q, z in enumerate(peers):
            out_copy(c, q, z, me_z).wait_send()
            out_copy(c, q, z, before[q]).wait_recv()
        out_own(c).wait()


def on_device(factors, screen, occ_energy, virt_energy):
    occ_g, virt, aux = factors.shape
    groups, shards = lax.axis_size("grp"), lax.axis_size("sh")
    rows = occ_g * virt
    per_block = rows // PIECE
    share = PIECE // shards
    slab = virt // shards
    span = groups // 4
    rounds = per_block * (span - 1) + per_block // 2
    batches = groups * per_block // 4
    turns = aux // (BLK * 4 if aux % (BLK * 4) == 0 else BLK)
    dma = pltpu.SemaphoreType.DMA
    bf16 = jnp.bfloat16
    smem = pl.BlockSpec(memory_space=pltpu.SMEM)
    return pl.pallas_call(
        functools.partial(amplitude_kernel, (occ_g, virt, aux, groups, shards)),
        out_shape=jax.ShapeDtypeStruct((occ_g, slab, aux * shards), bf16),
        in_specs=[pl.BlockSpec(memory_space=pl.ANY), smem, smem, pl.BlockSpec(memory_space=pltpu.VMEM)],
        out_specs=pl.BlockSpec(memory_space=pl.ANY),
        scratch_shapes=[
            pltpu.VMEM((groups * rows, aux), bf16),
            pltpu.VMEM((aux, rows), bf16),
            pltpu.VMEM((4 * PIECE, rows), jnp.float32),
            pltpu.VMEM((batches, shards, 4, share, rows), bf16),
            pltpu.VMEM((batches, shards - 1, 4, share, rows), bf16),
            pltpu.VMEM((batches, shards, 4, share, rows), bf16),
            pltpu.VMEM((virt, rows), jnp.float32),
            pltpu.VMEM((virt, virt), jnp.float32),
            pltpu.VMEM((groups * per_block, shards, share, virt), jnp.float32),
            pltpu.VMEM((rows, groups * rows), bf16),
            pltpu.VMEM((shards, occ_g, slab, aux), bf16),
            dma,
            dma((2, rounds)),
            dma((2, rounds)),
            dma((groups * per_block // 2,)),
            dma((groups * per_block // 2,)),
            dma((batches, shards - 1)),
            dma((batches, shards - 1)),
            dma((batches, shards - 1)),
            dma((batches, shards - 1)),
            dma((turns, shards - 1)),
            dma((turns, shards - 1)),
            dma((turns,)),
        ],
        cost_estimate=pl.CostEstimate(
            flops=4 * rows * groups * rows * aux, bytes_accessed=4 * rows * aux, transcendentals=0
        ),
        compiler_params=pltpu.CompilerParams(
            collective_id=0, has_side_effects=True, vmem_limit_bytes=56 * 1024 * 1024
        ),
    )(factors.reshape(rows, aux), screen, occ_energy, virt_energy.reshape(1, virt))


def solution(mesh):
    placed = (P("grp", None, "sh"), P("grp", None, "sh"), P(), P())
    return jax.shard_map(
        on_device, mesh=mesh, in_specs=placed, out_specs=P("grp", "sh", None), check_vma=False
    )
```

```python
import functools

import jax
import jax.numpy as jnp
from jax import lax
from jax.experimental import pallas as pl
from jax.experimental.pallas import tpu as pltpu
from jax.sharding import PartitionSpec as P

BLK = 128
PIECE = 64
WINDOW = 3
MESH = pl.DeviceIdType.MESH


def amplitude_kernel(
    dims, own_hbm, screen, occ_energy, virt_energy, out, blocks, own_t, part32, part16, arrived, sums, amp, tile32, turned,
    energy, weight, staged, own_sem, ring_send, ring_recv, twin_send, twin_recv, part_send, part_recv, amp_send,
    amp_recv, out_send, out_recv, out_local,
):
    occ_g, virt, aux, groups, shards = dims
    rows = occ_g * virt
    per_block = rows // PIECE
    per_orbital = virt // PIECE
    share = PIECE // shards
    slab = virt // shards
    chips = groups // 2
    span = chips // 2
    rounds = per_block * (span - 1) + per_block // 2
    levels = shards.bit_length() - 1
    me_g, me_z = lax.axis_index("grp"), lax.axis_index("sh")
    core = lax.rem(me_g, 2)
    chip = lax.div(me_g, 2)
    odd, line = lax.rem(chip, 2), lax.div(chip, 2)
    spot = line + odd * (chips - 1 - 2 * line)

    def at(offset, other):
        place = lax.rem(spot + offset + chips, chips)
        that = 2 * place + lax.div(place, span) * (2 * chips - 1 - 4 * place)
        return 2 * that + (1 - core if other else core)

    def rows_of(offset, other, chunk):
        return pl.ds(pl.multiple_of((per_block * at(offset, other) + chunk) * PIECE, PIECE), PIECE)

    right, left, twin = at(1, False), at(-1, False), at(0, True)
    peers = [lax.rem(me_z + q, shards) for q in range(1, shards)]
    before = [lax.rem(me_z - q + shards, shards) for q in range(1, shards)]

    own_rows = pl.ds(pl.multiple_of(me_g * rows, rows), rows)
    load = pltpu.make_async_copy(own_hbm, blocks.at[own_rows], own_sem)
    load.start()
    barrier = pltpu.get_barrier_semaphore()
    for g in (right, left, twin):
        pl.semaphore_signal(barrier, inc=1, device_id=(g, me_z), device_id_type=MESH)
    for z in peers:
        pl.semaphore_signal(barrier, inc=1, device_id=(me_g, z), device_id_type=MESH)
    load.wait()

    @pl.loop(0, aux // BLK)
    def _(p):
        columns = pl.ds(pl.multiple_of(p * BLK, BLK), BLK)
        for i in range(occ_g):
            keep = screen[i, 0, p].astype(jnp.float32)
            here = pl.ds(pl.multiple_of(me_g * rows + i * virt, virt), virt)
            blocks[here, columns] = (blocks[here, columns].astype(jnp.float32) * keep).astype(jnp.bfloat16)

    pl.semaphore_wait(barrier, 3 + shards - 1)

    sent = []

    def started(copy):
        copy.start()
        return copy

    def go(copy):
        sent.append(started(copy))

    def place_of(way, turn):
        step, rank = turn // per_block + 1, turn % per_block
        return step, (rank if way == 0 else per_block - 1 - rank)

    def ring(way, turn, receiving):
        step, chunk = place_of(way, turn)
        back = step if receiving else step - 1
        where = rows_of(-back if way == 0 else back, False, chunk)
        return pltpu.make_async_remote_copy(
            src_ref=blocks.at[where], dst_ref=blocks.at[where],
            send_sem=ring_send.at[way, turn], recv_sem=ring_recv.at[way, turn],
            device_id=(right if way == 0 else left, me_z), device_id_type=MESH,
        )

    def to_twin(offset, other, chunk, index):
        where = rows_of(offset, other, chunk)
        return pltpu.make_async_remote_copy(
            src_ref=blocks.at[where], dst_ref=blocks.at[where],
            send_sem=twin_send.at[index], recv_sem=twin_recv.at[index],
            device_id=(twin, me_z), device_id_type=MESH,
        )

    flying = {}
    for turn in range(min(WINDOW, rounds)):
        flying[turn] = [started(ring(way, turn, False)) for way in (0, 1)]
    for chunk in range(per_block):
        go(to_twin(0, False, chunk, chunk))

    depth = BLK * 4 if aux % (BLK * 4) == 0 else BLK

    @pl.loop(0, aux // depth)
    def _(k):
        at_k = pl.ds(pl.multiple_of(k * depth, depth), depth)
        own_t[at_k, :] = blocks[own_rows, at_k].astype(jnp.float32).T.astype(jnp.bfloat16)

    turned[...] = jnp.broadcast_to(virt_energy[...], (virt, virt)).T

    @pl.loop(0, groups * occ_g)
    def _(j):
        for part in range(per_orbital):
            for q in range(shards):
                low = part * PIECE + q * share
                energy[j * per_orbital + part, q] = turned[low:low + share, :] - occ_energy[j]

    own_energy = jnp.concatenate([virt_energy[...] - occ_energy[me_g * occ_g + i] for i in range(occ_g)], axis=1)

    def product(batch, number):
        part32[...] = jnp.zeros_like(part32)

        @pl.loop(0, aux // depth)
        def _(k):
            at_k = pl.ds(pl.multiple_of(k * depth, depth), depth)
            left_side = jnp.concatenate([blocks[rows_of(*entry), at_k] for entry in batch], axis=0)
            part32[...] += jnp.dot(left_side, own_t[at_k, :], preferred_element_type=jnp.float32)

        for c in range(len(batch)):
            for q in range(shards):
                low = c * PIECE + q * share
                part16[number, q, c] = part32[low:low + share, :].astype(jnp.bfloat16)
        halve(number, 0, part16, 0)

    bits = [lax.rem(lax.div(me_z, 1 << s), 2) for s in range(levels)]
    start = [0]
    for s in range(levels):
        start.append(start[s] + bits[s] * (shards >> (s + 1)))
    mine = start[levels]
    partner = [me_z + (1 - 2 * bits[s]) * (1 << s) for s in range(levels)]
    room = [shards - (shards >> s) for s in range(levels)]

    def halve(number, s, source, base):
        length = shards >> (s + 1)
        go(pltpu.make_async_remote_copy(
            src_ref=source.at[number, pl.ds(base + (1 - bits[s]) * length, length)],
            dst_ref=arrived.at[number, pl.ds(room[s], length)],
            send_sem=part_send.at[number, s], recv_sem=part_recv.at[number, s],
            device_id=(me_g, partner[s]), device_id_type=MESH,
        ))

    def halved(number, s):
        length = shards >> (s + 1)
        slot = arrived.at[number, pl.ds(room[s], length)]
        pltpu.make_async_copy(slot, slot, part_recv.at[number, s]).wait()
        source, base = (part16, 0) if s == 0 else (sums, room[s - 1])
        kept = source[number, pl.ds(base + bits[s] * length, length)].astype(jnp.float32)
        return kept + arrived[number, room[s]:room[s] + length].astype(jnp.float32)

    def double(number, s):
        held = amp.at[number, pl.ds(start[s + 1], shards >> (s + 1))]
        go(pltpu.make_async_remote_copy(
            src_ref=held, dst_ref=held, send_sem=amp_send.at[number, s], recv_sem=amp_recv.at[number, s],
            device_id=(me_g, partner[s]), device_id_type=MESH,
        ))

    def doubled(number, s):
        length = shards >> (s + 1)
        slot = amp.at[number, pl.ds(start[s] + (1 - bits[s]) * length, length)]
        pltpu.make_async_copy(slot, slot, amp_recv.at[number, s]).wait()

    def divide(batch, number):
        total = halved(number, levels - 1)
        for c, (offset, other, chunk) in enumerate(batch):
            theirs = energy[per_block * at(offset, other) + chunk, mine]
            gap = jnp.concatenate([theirs] * occ_g, axis=1) + own_energy
            amp[number, mine, c] = (total[0, c] / gap).astype(jnp.bfloat16)
        double(number, levels - 1)

    def stage(k, number):
        if k < levels:
            total = halved(number, k - 1)
            sums[number, room[k - 1]:room[k - 1] + (shards >> k)] = total.astype(jnp.bfloat16)
            halve(number, k, sums, room[k - 1])
        elif k == levels:
            divide(batches[number], number)
        else:
            doubled(number, 2 * levels - k)
            if k < 2 * levels:
                double(number, 2 * levels - k - 1)
            else:
                combine(batches[number], number)

    def tick(time):
        for k in range(2 * levels, 0, -1):
            if (time - k) % 2 == 0 and 0 <= time - k < 2 * len(batches):
                stage(k, (time - k) // 2)

    seen = {}

    def combine(batch, number):
        for c, (offset, other, chunk) in enumerate(batch):
            j = chunk // per_orbital
            key = (offset % chips, other, j)
            seen.setdefault(key, {})[chunk % per_orbital] = (number, c)
            if len(seen[key]) < per_orbital:
                continue
            for part, (n, at_c) in seen[key].items():
                for q in range(shards):
                    low = part * PIECE + q * share
                    tile32[low:low + share, :] = amp[n, q, at_c].astype(jnp.float32)
            columns = pl.ds(pl.multiple_of(at(offset, other) * rows + j * virt, virt), virt)
            for i in range(occ_g):
                tile = tile32[:, i * virt:(i + 1) * virt]
                weight[i * virt:(i + 1) * virt, columns] = (2.0 * tile.T - tile).astype(jnp.bfloat16)

    home = [(0, False, c) for c in range(per_block)] + [(0, True, c) for c in range(per_block)]
    first = len(home) // 4
    batches = []
    for number in range(first):
        batch = home[4 * number:4 * number + 4]
        for offset, other, chunk in batch:
            if other:
                to_twin(0, True, chunk, chunk).wait_recv()
        batches.append(batch)
        tick(2 * number)
        product(batch, number)
        tick(2 * number + 1)
    for turn in range(rounds):
        number = first + turn
        batch = []
        for way in (0, 1):
            step, chunk = place_of(way, turn)
            batch.append((-step if way == 0 else step, False, chunk))
        for way in (0, 1):
            ring(way, turn, True).wait_recv()
            go(to_twin(*batch[way], per_block + 2 * turn + way))
        for copy in flying[turn]:
            copy.wait_send()
        if turn + WINDOW < rounds:
            flying[turn + WINDOW] = [started(ring(way, turn + WINDOW, False)) for way in (0, 1)]
        tick(2 * number)
        for way in (0, 1):
            offset, _, chunk = batch[way]
            to_twin(offset, True, chunk, per_block + 2 * turn + way).wait_recv()
        batch = batch + [(offset, True, chunk) for offset, _, chunk in batch]
        batches.append(batch)
        product(batch, number)
        tick(2 * number + 1)
    for time in range(2 * len(batches), 2 * len(batches) + 2 * levels - 1):
        tick(time)

    wide = depth
    turns = aux // wide

    def out_copy(c, q, z, source):
        return pltpu.make_async_remote_copy(
            src_ref=staged.at[z, :, :, pl.ds(pl.multiple_of(c * wide, wide), wide)],
            dst_ref=out.at[:, :, pl.ds(pl.multiple_of(source * aux + c * wide, wide), wide)],
            send_sem=out_send.at[c, q], recv_sem=out_recv.at[c, q],
            device_id=(me_g, z), device_id_type=MESH,
        )

    def out_own(c):
        return pltpu.make_async_copy(
            staged.at[me_z, :, :, pl.ds(pl.multiple_of(c * wide, wide), wide)],
            out.at[:, :, pl.ds(pl.multiple_of(me_z * aux + c * wide, wide), wide)],
            out_local.at[c],
        )

    @pl.loop(0, turns)
    def _(c):
        here = pl.ds(pl.multiple_of(c * wide, wide), wide)
        gamma = jnp.dot(weight[...], blocks[:, here], preferred_element_type=jnp.float32)
        for i in range(occ_g):
            for q in range(shards):
                low = i * virt + q * slab
                staged[q, i, :, here] = gamma[low:low + slab, :].astype(jnp.bfloat16)
        for q, z in enumerate(peers):
            out_copy(c, q, z, me_z).start()
        out_own(c).start()

    for copy in sent:
        copy.wait_send()

    @pl.loop(0, turns)
    def _(c):
        for q, z in enumerate(peers):
            out_copy(c, q, z, me_z).wait_send()
            out_copy(c, q, z, before[q]).wait_recv()
        out_own(c).wait()


def on_device(factors, screen, occ_energy, virt_energy):
    occ_g, virt, aux = factors.shape
    groups, shards = lax.axis_size("grp"), lax.axis_size("sh")
    rows = occ_g * virt
    per_block = rows // PIECE
    share = PIECE // shards
    slab = virt // shards
    span = groups // 4
    rounds = per_block * (span - 1) + per_block // 2
    levels = shards.bit_length() - 1
    batches = groups * per_block // 4
    turns = aux // (BLK * 4 if aux % (BLK * 4) == 0 else BLK)
    dma = pltpu.SemaphoreType.DMA
    bf16 = jnp.bfloat16
    smem = pl.BlockSpec(memory_space=pltpu.SMEM)
    return pl.pallas_call(
        functools.partial(amplitude_kernel, (occ_g, virt, aux, groups, shards)),
        out_shape=jax.ShapeDtypeStruct((occ_g, slab, aux * shards), bf16),
        in_specs=[pl.BlockSpec(memory_space=pl.ANY), smem, smem, pl.BlockSpec(memory_space=pltpu.VMEM)],
        out_specs=pl.BlockSpec(memory_space=pl.ANY),
        scratch_shapes=[
            pltpu.VMEM((groups * rows, aux), bf16),
            pltpu.VMEM((aux, rows), bf16),
            pltpu.VMEM((4 * PIECE, rows), jnp.float32),
            pltpu.VMEM((batches, shards, 4, share, rows), bf16),
            pltpu.VMEM((batches, shards - 1, 4, share, rows), bf16),
            pltpu.VMEM((batches, shards - 1, 4, share, rows), bf16),
            pltpu.VMEM((batches, shards, 4, share, rows), bf16),
            pltpu.VMEM((virt, rows), jnp.float32),
            pltpu.VMEM((virt, virt), jnp.float32),
            pltpu.VMEM((groups * per_block, shards, share, virt), jnp.float32),
            pltpu.VMEM((rows, groups * rows), bf16),
            pltpu.VMEM((shards, occ_g, slab, aux), bf16),
            dma,
            dma((2, rounds)),
            dma((2, rounds)),
            dma((groups * per_block // 2,)),
            dma((groups * per_block // 2,)),
            dma((batches, levels)),
            dma((batches, levels)),
            dma((batches, levels)),
            dma((batches, levels)),
            dma((turns, shards - 1)),
            dma((turns, shards - 1)),
            dma((turns,)),
        ],
        cost_estimate=pl.CostEstimate(
            flops=4 * rows * groups * rows * aux, bytes_accessed=4 * rows * aux, transcendentals=0
        ),
        compiler_params=pltpu.CompilerParams(
            collective_id=0, has_side_effects=True, vmem_limit_bytes=56 * 1024 * 1024
        ),
    )(factors.reshape(rows, aux), screen, occ_energy, virt_energy.reshape(1, virt))


def solution(mesh):
    placed = (P("grp", None, "sh"), P("grp", None, "sh"), P(), P())
    return jax.shard_map(
        on_device, mesh=mesh, in_specs=placed, out_specs=P("grp", "sh", None), check_vma=False
    )
```

```python
import functools

import jax
import jax.numpy as jnp
from jax import lax
from jax.experimental import pallas as pl
from jax.experimental.pallas import tpu as pltpu
from jax.sharding import PartitionSpec as P

BLK = 128
PIECE = 64
WINDOW = 4
MESH = pl.DeviceIdType.MESH


def amplitude_kernel(
    dims, own_hbm, screen, occ_energy, virt_energy, out, blocks, own_t, part32, part16, arrived, amp, tile32, turned,
    energy, weight, staged, own_sem, ring_send, ring_recv, twin_send, twin_recv, part_send, part_recv, amp_send,
    amp_recv, out_send, out_recv, out_local,
):
    occ_g, virt, aux, groups, shards = dims
    rows = occ_g * virt
    per_block = rows // PIECE
    per_orbital = virt // PIECE
    share = PIECE // shards
    slab = virt // shards
    chips = groups // 2
    span = chips // 2
    rounds = per_block * (span - 1) + per_block // 2
    me_g, me_z = lax.axis_index("grp"), lax.axis_index("sh")
    core = lax.rem(me_g, 2)
    chip = lax.div(me_g, 2)
    odd, line = lax.rem(chip, 2), lax.div(chip, 2)
    spot = line + odd * (chips - 1 - 2 * line)

    def at(offset, other):
        place = lax.rem(spot + offset + chips, chips)
        that = 2 * place + lax.div(place, span) * (2 * chips - 1 - 4 * place)
        return 2 * that + (1 - core if other else core)

    def rows_of(offset, other, chunk):
        return pl.ds(pl.multiple_of((per_block * at(offset, other) + chunk) * PIECE, PIECE), PIECE)

    right, left, twin = at(1, False), at(-1, False), at(0, True)
    peers = [lax.rem(me_z + q, shards) for q in range(1, shards)]
    before = [lax.rem(me_z - q + shards, shards) for q in range(1, shards)]

    own_rows = pl.ds(pl.multiple_of(me_g * rows, rows), rows)
    load = pltpu.make_async_copy(own_hbm, blocks.at[own_rows], own_sem)
    load.start()
    barrier = pltpu.get_barrier_semaphore()
    for g in (right, left, twin):
        pl.semaphore_signal(barrier, inc=1, device_id=(g, me_z), device_id_type=MESH)
    for z in peers:
        pl.semaphore_signal(barrier, inc=1, device_id=(me_g, z), device_id_type=MESH)
    load.wait()

    @pl.loop(0, aux // BLK)
    def _(p):
        columns = pl.ds(pl.multiple_of(p * BLK, BLK), BLK)
        for i in range(occ_g):
            keep = screen[i, 0, p].astype(jnp.float32)
            here = pl.ds(pl.multiple_of(me_g * rows + i * virt, virt), virt)
            blocks[here, columns] = (blocks[here, columns].astype(jnp.float32) * keep).astype(jnp.bfloat16)

    pl.semaphore_wait(barrier, 3 + shards - 1)

    sent = []

    def started(copy):
        copy.start()
        return copy

    def go(copy):
        sent.append(started(copy))

    def place_of(way, turn):
        step, rank = turn // per_block + 1, turn % per_block
        return step, (rank if way == 0 else per_block - 1 - rank)

    def ring(way, turn, receiving):
        step, chunk = place_of(way, turn)
        back = step if receiving else step - 1
        where = rows_of(-back if way == 0 else back, False, chunk)
        return pltpu.make_async_remote_copy(
            src_ref=blocks.at[where], dst_ref=blocks.at[where],
            send_sem=ring_send.at[way, turn], recv_sem=ring_recv.at[way, turn],
            device_id=(right if way == 0 else left, me_z), device_id_type=MESH,
        )

    def to_twin(offset, other, chunk, index):
        where = rows_of(offset, other, chunk)
        return pltpu.make_async_remote_copy(
            src_ref=blocks.at[where], dst_ref=blocks.at[where],
            send_sem=twin_send.at[index], recv_sem=twin_recv.at[index],
            device_id=(twin, me_z), device_id_type=MESH,
        )

    flying = {}
    for turn in range(min(WINDOW, rounds)):
        flying[turn] = [started(ring(way, turn, False)) for way in (0, 1)]
    for chunk in range(per_block):
        go(to_twin(0, False, chunk, chunk))

    depth = BLK * 4 if aux % (BLK * 4) == 0 else BLK

    @pl.loop(0, aux // depth)
    def _(k):
        at_k = pl.ds(pl.multiple_of(k * depth, depth), depth)
        own_t[at_k, :] = blocks[own_rows, at_k].astype(jnp.float32).T.astype(jnp.bfloat16)

    turned[...] = jnp.broadcast_to(virt_energy[...], (virt, virt)).T

    @pl.loop(0, groups * occ_g)
    def _(j):
        for part in range(per_orbital):
            for q in range(shards):
                low = part * PIECE + q * share
                energy[j * per_orbital + part, q] = turned[low:low + share, :] - occ_energy[j]

    own_energy = jnp.concatenate([virt_energy[...] - occ_energy[me_g * occ_g + i] for i in range(occ_g)], axis=1)

    def product(batch, number):
        part32[...] = jnp.zeros_like(part32)

        @pl.loop(0, aux // depth)
        def _(k):
            at_k = pl.ds(pl.multiple_of(k * depth, depth), depth)
            left_side = jnp.concatenate([blocks[rows_of(*entry), at_k] for entry in batch], axis=0)
            part32[...] += jnp.dot(left_side, own_t[at_k, :], preferred_element_type=jnp.float32)

        for c in range(len(batch)):
            for q in range(shards):
                low = c * PIECE + q * share
                part16[number, q, c] = part32[low:low + share, :].astype(jnp.bfloat16)
        for q, z in enumerate(peers):
            go(pltpu.make_async_remote_copy(
                src_ref=part16.at[number, z], dst_ref=arrived.at[number, q],
                send_sem=part_send.at[number, q], recv_sem=part_recv.at[number, q],
                device_id=(me_g, z), device_id_type=MESH,
            ))

    def divide(batch, number):
        for q in range(shards - 1):
            pltpu.make_async_copy(arrived.at[number, q], arrived.at[number, q], part_recv.at[number, q]).wait()
        for c, (offset, other, chunk) in enumerate(batch):
            total = part16[number, me_z, c].astype(jnp.float32)
            for q in range(shards - 1):
                total += arrived[number, q, c].astype(jnp.float32)
            theirs = energy[per_block * at(offset, other) + chunk, me_z]
            gap = jnp.concatenate([theirs] * occ_g, axis=1) + own_energy
            amp[number, me_z, c] = (total / gap).astype(jnp.bfloat16)
        for q, z in enumerate(peers):
            go(pltpu.make_async_remote_copy(
                src_ref=amp.at[number, me_z], dst_ref=amp.at[number, me_z],
                send_sem=amp_send.at[number, q], recv_sem=amp_recv.at[number, q],
                device_id=(me_g, z), device_id_type=MESH,
            ))

    seen = {}

    def combine(batch, number):
        for q, z in enumerate(before):
            slot = amp.at[number, z]
            pltpu.make_async_copy(slot, slot, amp_recv.at[number, q]).wait()
        for c, (offset, other, chunk) in enumerate(batch):
            j = chunk // per_orbital
            key = (offset % chips, other, j)
            seen.setdefault(key, {})[chunk % per_orbital] = (number, c)
            if len(seen[key]) < per_orbital:
                continue
            for part, (n, at_c) in seen[key].items():
                for q in range(shards):
                    low = part * PIECE + q * share
                    tile32[low:low + share, :] = amp[n, q, at_c].astype(jnp.float32)
            columns = pl.ds(pl.multiple_of(at(offset, other) * rows + j * virt, virt), virt)
            for i in range(occ_g):
                tile = tile32[:, i * virt:(i + 1) * virt]
                weight[i * virt:(i + 1) * virt, columns] = (2.0 * tile.T - tile).astype(jnp.bfloat16)

    home = [(0, False, c) for c in range(per_block)] + [(0, True, c) for c in range(per_block)]
    batches = [home[b:b + 4] for b in range(0, len(home), 4)]
    first = len(batches)
    for number, batch in enumerate(batches):
        for offset, other, chunk in batch:
            if other:
                to_twin(0, True, chunk, chunk).wait_recv()
        product(batch, number)
        if number >= 1:
            divide(batches[number - 1], number - 1)
        if number >= 2:
            combine(batches[number - 2], number - 2)
    for turn in range(rounds):
        number = first + turn
        batch = []
        for way in (0, 1):
            step, chunk = place_of(way, turn)
            batch.append((-step if way == 0 else step, False, chunk))
        for way in (0, 1):
            ring(way, turn, True).wait_recv()
            go(to_twin(*batch[way], per_block + 2 * turn + way))
        for copy in flying[turn]:
            copy.wait_send()
        if turn + WINDOW < rounds:
            flying[turn + WINDOW] = [started(ring(way, turn + WINDOW, False)) for way in (0, 1)]
        divide(batches[number - 1], number - 1)
        for way in (0, 1):
            offset, _, chunk = batch[way]
            to_twin(offset, True, chunk, per_block + 2 * turn + way).wait_recv()
        batch = batch + [(offset, True, chunk) for offset, _, chunk in batch]
        batches.append(batch)
        product(batch, number)
        if number >= 2:
            combine(batches[number - 2], number - 2)
    last = len(batches) - 1
    divide(batches[last], last)
    combine(batches[last - 1], last - 1)
    combine(batches[last], last)

    wide = BLK * 2 if aux % (BLK * 2) == 0 else BLK
    turns = aux // wide

    def out_copy(c, q, z, source):
        return pltpu.make_async_remote_copy(
            src_ref=staged.at[z, :, :, pl.ds(pl.multiple_of(c * wide, wide), wide)],
            dst_ref=out.at[:, :, pl.ds(pl.multiple_of(source * aux + c * wide, wide), wide)],
            send_sem=out_send.at[c, q], recv_sem=out_recv.at[c, q],
            device_id=(me_g, z), device_id_type=MESH,
        )

    def out_own(c):
        return pltpu.make_async_copy(
            staged.at[me_z, :, :, pl.ds(pl.multiple_of(c * wide, wide), wide)],
            out.at[:, :, pl.ds(pl.multiple_of(me_z * aux + c * wide, wide), wide)],
            out_local.at[c],
        )

    @pl.loop(0, turns)
    def _(c):
        here = pl.ds(pl.multiple_of(c * wide, wide), wide)
        gamma = jnp.dot(weight[...], blocks[:, here], preferred_element_type=jnp.float32)
        for i in range(occ_g):
            for q in range(shards):
                low = i * virt + q * slab
                staged[q, i, :, here] = gamma[low:low + slab, :].astype(jnp.bfloat16)
        for q, z in enumerate(peers):
            out_copy(c, q, z, me_z).start()
        out_own(c).start()

    for copy in sent:
        copy.wait_send()

    @pl.loop(0, turns)
    def _(c):
        for q, z in enumerate(peers):
            out_copy(c, q, z, me_z).wait_send()
            out_copy(c, q, z, before[q]).wait_recv()
        out_own(c).wait()


def on_device(factors, screen, occ_energy, virt_energy):
    occ_g, virt, aux = factors.shape
    groups, shards = lax.axis_size("grp"), lax.axis_size("sh")
    rows = occ_g * virt
    per_block = rows // PIECE
    share = PIECE // shards
    slab = virt // shards
    span = groups // 4
    rounds = per_block * (span - 1) + per_block // 2
    batches = groups * per_block // 4
    turns = aux // (BLK * 2 if aux % (BLK * 2) == 0 else BLK)
    dma = pltpu.SemaphoreType.DMA
    bf16 = jnp.bfloat16
    smem = pl.BlockSpec(memory_space=pltpu.SMEM)
    return pl.pallas_call(
        functools.partial(amplitude_kernel, (occ_g, virt, aux, groups, shards)),
        out_shape=jax.ShapeDtypeStruct((occ_g, slab, aux * shards), bf16),
        in_specs=[pl.BlockSpec(memory_space=pl.ANY), smem, smem, pl.BlockSpec(memory_space=pltpu.VMEM)],
        out_specs=pl.BlockSpec(memory_space=pl.ANY),
        scratch_shapes=[
            pltpu.VMEM((groups * rows, aux), bf16),
            pltpu.VMEM((aux, rows), bf16),
            pltpu.VMEM((4 * PIECE, rows), jnp.float32),
            pltpu.VMEM((batches, shards, 4, share, rows), bf16),
            pltpu.VMEM((batches, shards - 1, 4, share, rows), bf16),
            pltpu.VMEM((batches, shards, 4, share, rows), bf16),
            pltpu.VMEM((virt, rows), jnp.float32),
            pltpu.VMEM((virt, virt), jnp.float32),
            pltpu.VMEM((groups * per_block, shards, share, virt), jnp.float32),
            pltpu.VMEM((rows, groups * rows), bf16),
            pltpu.VMEM((shards, occ_g, slab, aux), bf16),
            dma,
            dma((2, rounds)),
            dma((2, rounds)),
            dma((groups * per_block // 2,)),
            dma((groups * per_block // 2,)),
            dma((batches, shards - 1)),
            dma((batches, shards - 1)),
            dma((batches, shards - 1)),
            dma((batches, shards - 1)),
            dma((turns, shards - 1)),
            dma((turns, shards - 1)),
            dma((turns,)),
        ],
        cost_estimate=pl.CostEstimate(
            flops=4 * rows * groups * rows * aux, bytes_accessed=4 * rows * aux, transcendentals=0
        ),
        compiler_params=pltpu.CompilerParams(
            collective_id=0, has_side_effects=True, vmem_limit_bytes=56 * 1024 * 1024
        ),
    )(factors.reshape(rows, aux), screen, occ_energy, virt_energy.reshape(1, virt))


def solution(mesh):
    placed = (P("grp", None, "sh"), P("grp", None, "sh"), P(), P())
    return jax.shard_map(
        on_device, mesh=mesh, in_specs=placed, out_specs=P("grp", "sh", None), check_vma=False
    )
```

```python
import functools

import jax
import jax.numpy as jnp
from jax import lax
from jax.experimental import pallas as pl
from jax.experimental.pallas import tpu as pltpu
from jax.sharding import PartitionSpec as P

BLK = 128
PIECE = 64
WINDOW = 3
MESH = pl.DeviceIdType.MESH


def amplitude_kernel(
    dims, own_hbm, screen, occ_energy, virt_energy, out, blocks, own_t, part32, part16, arrived, amp, tile32, turned,
    energy, weight, staged, own_sem, ring_send, ring_recv, twin_send, twin_recv, part_send, part_recv, amp_send,
    amp_recv, out_send, out_recv, out_local,
):
    occ_g, virt, aux, groups, shards = dims
    rows = occ_g * virt
    per_block = rows // PIECE
    per_orbital = virt // PIECE
    share = PIECE // shards
    slab = virt // shards
    chips = groups // 2
    span = chips // 2
    rounds = per_block * (span - 1) + per_block // 2
    me_g, me_z = lax.axis_index("grp"), lax.axis_index("sh")
    core = lax.rem(me_g, 2)
    chip = lax.div(me_g, 2)
    odd, line = lax.rem(chip, 2), lax.div(chip, 2)
    spot = line + odd * (chips - 1 - 2 * line)

    def at(offset, other):
        place = lax.rem(spot + offset + chips, chips)
        that = 2 * place + lax.div(place, span) * (2 * chips - 1 - 4 * place)
        return 2 * that + (1 - core if other else core)

    def rows_of(offset, other, chunk):
        return pl.ds(pl.multiple_of((per_block * at(offset, other) + chunk) * PIECE, PIECE), PIECE)

    right, left, twin = at(1, False), at(-1, False), at(0, True)
    peers = [lax.rem(me_z + q, shards) for q in range(1, shards)]
    before = [lax.rem(me_z - q + shards, shards) for q in range(1, shards)]

    own_rows = pl.ds(pl.multiple_of(me_g * rows, rows), rows)
    order = [c for pair in zip(range(per_block // 2), range(per_block - 1, -1, -1)) for c in pair]

    def load(chunk):
        return pltpu.make_async_copy(
            own_hbm.at[pl.ds(chunk * PIECE, PIECE)], blocks.at[rows_of(0, False, chunk)], own_sem.at[chunk]
        )

    for chunk in order:
        load(chunk).start()
    barrier = pltpu.get_barrier_semaphore()
    for g in (right, left, twin):
        pl.semaphore_signal(barrier, inc=1, device_id=(g, me_z), device_id_type=MESH)
    for z in peers:
        pl.semaphore_signal(barrier, inc=1, device_id=(me_g, z), device_id_type=MESH)

    def masked(chunk):
        load(chunk).wait()

        @pl.loop(0, aux // BLK)
        def _(p):
            columns = pl.ds(pl.multiple_of(p * BLK, BLK), BLK)
            keep = screen[chunk // per_orbital, 0, p].astype(jnp.float32)
            here = rows_of(0, False, chunk)
            blocks[here, columns] = (blocks[here, columns].astype(jnp.float32) * keep).astype(jnp.bfloat16)

    for chunk in order[:2]:
        masked(chunk)
    pl.semaphore_wait(barrier, 3 + shards - 1)

    sent = []

    def started(copy):
        copy.start()
        return copy

    def go(copy):
        sent.append(started(copy))

    def place_of(way, turn):
        step, rank = turn // per_block + 1, turn % per_block
        return step, (rank if way == 0 else per_block - 1 - rank)

    def ring(way, turn, receiving):
        step, chunk = place_of(way, turn)
        back = step if receiving else step - 1
        where = rows_of(-back if way == 0 else back, False, chunk)
        return pltpu.make_async_remote_copy(
            src_ref=blocks.at[where], dst_ref=blocks.at[where],
            send_sem=ring_send.at[way, turn], recv_sem=ring_recv.at[way, turn],
            device_id=(right if way == 0 else left, me_z), device_id_type=MESH,
        )

    def to_twin(offset, other, chunk, index):
        where = rows_of(offset, other, chunk)
        return pltpu.make_async_remote_copy(
            src_ref=blocks.at[where], dst_ref=blocks.at[where],
            send_sem=twin_send.at[index], recv_sem=twin_recv.at[index],
            device_id=(twin, me_z), device_id_type=MESH,
        )

    flying = {}
    for turn in range(per_block):
        if turn >= 1 and 2 * turn < per_block:
            masked(order[2 * turn])
            masked(order[2 * turn + 1])
        if turn < min(WINDOW, rounds):
            flying[turn] = [started(ring(way, turn, False)) for way in (0, 1)]
    for chunk in range(per_block):
        go(to_twin(0, False, chunk, chunk))

    depth = BLK * 4 if aux % (BLK * 4) == 0 else BLK

    @pl.loop(0, aux // depth)
    def _(k):
        at_k = pl.ds(pl.multiple_of(k * depth, depth), depth)
        own_t[at_k, :] = blocks[own_rows, at_k].astype(jnp.float32).T.astype(jnp.bfloat16)

    turned[...] = jnp.broadcast_to(virt_energy[...], (virt, virt)).T

    @pl.loop(0, groups * occ_g)
    def _(j):
        for part in range(per_orbital):
            for q in range(shards):
                low = part * PIECE + q * share
                energy[j * per_orbital + part, q] = turned[low:low + share, :] - occ_energy[j]

    own_energy = jnp.concatenate([virt_energy[...] - occ_energy[me_g * occ_g + i] for i in range(occ_g)], axis=1)

    def product(batch, number):
        part32[...] = jnp.zeros_like(part32)

        @pl.loop(0, aux // depth)
        def _(k):
            at_k = pl.ds(pl.multiple_of(k * depth, depth), depth)
            left_side = jnp.concatenate([blocks[rows_of(*entry), at_k] for entry in batch], axis=0)
            part32[...] += jnp.dot(left_side, own_t[at_k, :], preferred_element_type=jnp.float32)

        for c in range(len(batch)):
            for q in range(shards):
                low = c * PIECE + q * share
                part16[number, q, c] = part32[low:low + share, :].astype(jnp.bfloat16)
        for q, z in enumerate(peers):
            go(pltpu.make_async_remote_copy(
                src_ref=part16.at[number, z], dst_ref=arrived.at[number, q],
                send_sem=part_send.at[number, q], recv_sem=part_recv.at[number, q],
                device_id=(me_g, z), device_id_type=MESH,
            ))

    def divide(batch, number):
        for q in range(shards - 1):
            pltpu.make_async_copy(arrived.at[number, q], arrived.at[number, q], part_recv.at[number, q]).wait()
        for c, (offset, other, chunk) in enumerate(batch):
            total = part16[number, me_z, c].astype(jnp.float32)
            for q in range(shards - 1):
                total += arrived[number, q, c].astype(jnp.float32)
            theirs = energy[per_block * at(offset, other) + chunk, me_z]
            gap = jnp.concatenate([theirs] * occ_g, axis=1) + own_energy
            amp[number, me_z, c] = (total / gap).astype(jnp.bfloat16)
        for q, z in enumerate(peers):
            go(pltpu.make_async_remote_copy(
                src_ref=amp.at[number, me_z], dst_ref=amp.at[number, me_z],
                send_sem=amp_send.at[number, q], recv_sem=amp_recv.at[number, q],
                device_id=(me_g, z), device_id_type=MESH,
            ))

    seen = {}

    def combine(batch, number):
        for q, z in enumerate(before):
            slot = amp.at[number, z]
            pltpu.make_async_copy(slot, slot, amp_recv.at[number, q]).wait()
        for c, (offset, other, chunk) in enumerate(batch):
            j = chunk // per_orbital
            key = (offset % chips, other, j)
            seen.setdefault(key, {})[chunk % per_orbital] = (number, c)
            if len(seen[key]) < per_orbital:
                continue
            for part, (n, at_c) in seen[key].items():
                for q in range(shards):
                    low = part * PIECE + q * share
                    tile32[low:low + share, :] = amp[n, q, at_c].astype(jnp.float32)
            columns = pl.ds(pl.multiple_of(at(offset, other) * rows + j * virt, virt), virt)
            for i in range(occ_g):
                tile = tile32[:, i * virt:(i + 1) * virt]
                weight[i * virt:(i + 1) * virt, columns] = (2.0 * tile.T - tile).astype(jnp.bfloat16)

    home = [(0, False, c) for c in range(per_block)] + [(0, True, c) for c in range(per_block)]
    batches = [home[b:b + 4] for b in range(0, len(home), 4)]
    first = len(batches)
    for number, batch in enumerate(batches):
        for offset, other, chunk in batch:
            if other:
                to_twin(0, True, chunk, chunk).wait_recv()
        product(batch, number)
        if number >= 1:
            divide(batches[number - 1], number - 1)
        if number >= 2:
            combine(batches[number - 2], number - 2)
    for turn in range(rounds):
        number = first + turn
        batch = []
        for way in (0, 1):
            step, chunk = place_of(way, turn)
            batch.append((-step if way == 0 else step, False, chunk))
        for way in (0, 1):
            ring(way, turn, True).wait_recv()
            go(to_twin(*batch[way], per_block + 2 * turn + way))
        for copy in flying[turn]:
            copy.wait_send()
        if turn + WINDOW < rounds:
            flying[turn + WINDOW] = [started(ring(way, turn + WINDOW, False)) for way in (0, 1)]
        divide(batches[number - 1], number - 1)
        for way in (0, 1):
            offset, _, chunk = batch[way]
            to_twin(offset, True, chunk, per_block + 2 * turn + way).wait_recv()
        batch = batch + [(offset, True, chunk) for offset, _, chunk in batch]
        batches.append(batch)
        product(batch, number)
        if number >= 2:
            combine(batches[number - 2], number - 2)
    last = len(batches) - 1
    combine(batches[last - 1], last - 1)
    divide(batches[last], last)
    combine(batches[last], last)

    wide = depth
    turns = aux // wide

    def out_copy(c, q, z, source):
        return pltpu.make_async_remote_copy(
            src_ref=staged.at[z, :, :, pl.ds(pl.multiple_of(c * wide, wide), wide)],
            dst_ref=out.at[:, :, pl.ds(pl.multiple_of(source * aux + c * wide, wide), wide)],
            send_sem=out_send.at[c, q], recv_sem=out_recv.at[c, q],
            device_id=(me_g, z), device_id_type=MESH,
        )

    def out_own(c):
        return pltpu.make_async_copy(
            staged.at[me_z, :, :, pl.ds(pl.multiple_of(c * wide, wide), wide)],
            out.at[:, :, pl.ds(pl.multiple_of(me_z * aux + c * wide, wide), wide)],
            out_local.at[c],
        )

    @pl.loop(0, turns)
    def _(c):
        here = pl.ds(pl.multiple_of(c * wide, wide), wide)
        gamma = jnp.dot(weight[...], blocks[:, here], preferred_element_type=jnp.float32)
        for i in range(occ_g):
            for q in range(shards):
                low = i * virt + q * slab
                staged[q, i, :, here] = gamma[low:low + slab, :].astype(jnp.bfloat16)
        for q, z in enumerate(peers):
            out_copy(c, q, z, me_z).start()
        out_own(c).start()

    for copy in sent:
        copy.wait_send()

    @pl.loop(0, turns)
    def _(c):
        for q, z in enumerate(peers):
            out_copy(c, q, z, me_z).wait_send()
            out_copy(c, q, z, before[q]).wait_recv()
        out_own(c).wait()


def on_device(factors, screen, occ_energy, virt_energy):
    occ_g, virt, aux = factors.shape
    groups, shards = lax.axis_size("grp"), lax.axis_size("sh")
    rows = occ_g * virt
    per_block = rows // PIECE
    share = PIECE // shards
    slab = virt // shards
    span = groups // 4
    rounds = per_block * (span - 1) + per_block // 2
    batches = groups * per_block // 4
    turns = aux // (BLK * 4 if aux % (BLK * 4) == 0 else BLK)
    dma = pltpu.SemaphoreType.DMA
    bf16 = jnp.bfloat16
    smem = pl.BlockSpec(memory_space=pltpu.SMEM)
    return pl.pallas_call(
        functools.partial(amplitude_kernel, (occ_g, virt, aux, groups, shards)),
        out_shape=jax.ShapeDtypeStruct((occ_g, slab, aux * shards), bf16),
        in_specs=[pl.BlockSpec(memory_space=pl.ANY), smem, smem, pl.BlockSpec(memory_space=pltpu.VMEM)],
        out_specs=pl.BlockSpec(memory_space=pl.ANY),
        scratch_shapes=[
            pltpu.VMEM((groups * rows, aux), bf16),
            pltpu.VMEM((aux, rows), bf16),
            pltpu.VMEM((4 * PIECE, rows), jnp.float32),
            pltpu.VMEM((batches, shards, 4, share, rows), bf16),
            pltpu.VMEM((batches, shards - 1, 4, share, rows), bf16),
            pltpu.VMEM((batches, shards, 4, share, rows), bf16),
            pltpu.VMEM((virt, rows), jnp.float32),
            pltpu.VMEM((virt, virt), jnp.float32),
            pltpu.VMEM((groups * per_block, shards, share, virt), jnp.float32),
            pltpu.VMEM((rows, groups * rows), bf16),
            pltpu.VMEM((shards, occ_g, slab, aux), bf16),
            dma((per_block,)),
            dma((2, rounds)),
            dma((2, rounds)),
            dma((groups * per_block // 2,)),
            dma((groups * per_block // 2,)),
            dma((batches, shards - 1)),
            dma((batches, shards - 1)),
            dma((batches, shards - 1)),
            dma((batches, shards - 1)),
            dma((turns, shards - 1)),
            dma((turns, shards - 1)),
            dma((turns,)),
        ],
        cost_estimate=pl.CostEstimate(
            flops=4 * rows * groups * rows * aux, bytes_accessed=4 * rows * aux, transcendentals=0
        ),
        compiler_params=pltpu.CompilerParams(
            collective_id=0, has_side_effects=True, vmem_limit_bytes=56 * 1024 * 1024
        ),
    )(factors.reshape(rows, aux), screen, occ_energy, virt_energy.reshape(1, virt))


def solution(mesh):
    placed = (P("grp", None, "sh"), P("grp", None, "sh"), P(), P())
    return jax.shard_map(
        on_device, mesh=mesh, in_specs=placed, out_specs=P("grp", "sh", None), check_vma=False
    )
```

```python
import functools

import jax
import jax.numpy as jnp
from jax import lax
from jax.experimental import pallas as pl
from jax.experimental.pallas import tpu as pltpu
from jax.sharding import PartitionSpec as P

BLK = 128
PIECE = 64
WINDOW = 3
MESH = pl.DeviceIdType.MESH


def amplitude_kernel(
    dims, own_hbm, screen, occ_energy, virt_energy, out, blocks, own_t, part32, part16, arrived, amp, tile32, turned,
    energy, weight, staged, own_sem, ring_send, ring_recv, twin_send, twin_recv, part_send, part_recv, amp_send,
    amp_recv, out_send, out_recv, out_local,
):
    occ_g, virt, aux, groups, shards = dims
    rows = occ_g * virt
    per_block = rows // PIECE
    per_orbital = virt // PIECE
    share = PIECE // shards
    slab = virt // shards
    chips = groups // 2
    span = chips // 2
    rounds = per_block * (span - 1) + per_block // 2
    me_g, me_z = lax.axis_index("grp"), lax.axis_index("sh")
    core = lax.rem(me_g, 2)
    chip = lax.div(me_g, 2)
    odd, line = lax.rem(chip, 2), lax.div(chip, 2)
    spot = line + odd * (chips - 1 - 2 * line)

    def at(offset, other):
        place = lax.rem(spot + offset + chips, chips)
        that = 2 * place + lax.div(place, span) * (2 * chips - 1 - 4 * place)
        return 2 * that + (1 - core if other else core)

    def rows_of(offset, other, chunk):
        return pl.ds(pl.multiple_of((per_block * at(offset, other) + chunk) * PIECE, PIECE), PIECE)

    right, left, twin = at(1, False), at(-1, False), at(0, True)
    peers = [lax.rem(me_z + q, shards) for q in range(1, shards)]
    before = [lax.rem(me_z - q + shards, shards) for q in range(1, shards)]

    own_rows = pl.ds(pl.multiple_of(me_g * rows, rows), rows)
    order = [c for pair in zip(range(per_block // 2), range(per_block - 1, -1, -1)) for c in pair]

    def load(chunk):
        return pltpu.make_async_copy(
            own_hbm.at[pl.ds(chunk * PIECE, PIECE)], blocks.at[rows_of(0, False, chunk)], own_sem.at[chunk]
        )

    for chunk in order:
        load(chunk).start()
    barrier = pltpu.get_barrier_semaphore()
    for g in (right, left, twin):
        pl.semaphore_signal(barrier, inc=1, device_id=(g, me_z), device_id_type=MESH)
    for z in peers:
        pl.semaphore_signal(barrier, inc=1, device_id=(me_g, z), device_id_type=MESH)

    def masked(chunk):
        load(chunk).wait()

        @pl.loop(0, aux // BLK)
        def _(p):
            columns = pl.ds(pl.multiple_of(p * BLK, BLK), BLK)
            keep = screen[chunk // per_orbital, 0, p].astype(jnp.float32)
            here = rows_of(0, False, chunk)
            blocks[here, columns] = (blocks[here, columns].astype(jnp.float32) * keep).astype(jnp.bfloat16)

    for chunk in order[:2]:
        masked(chunk)
    pl.semaphore_wait(barrier, 3 + shards - 1)

    sent = []

    def started(copy):
        copy.start()
        return copy

    def go(copy):
        sent.append(started(copy))

    def place_of(way, turn):
        step, rank = turn // per_block + 1, turn % per_block
        return step, (rank if way == 0 else per_block - 1 - rank)

    def ring(way, turn, receiving):
        step, chunk = place_of(way, turn)
        back = step if receiving else step - 1
        where = rows_of(-back if way == 0 else back, False, chunk)
        return pltpu.make_async_remote_copy(
            src_ref=blocks.at[where], dst_ref=blocks.at[where],
            send_sem=ring_send.at[way, turn], recv_sem=ring_recv.at[way, turn],
            device_id=(right if way == 0 else left, me_z), device_id_type=MESH,
        )

    def to_twin(offset, other, chunk, index):
        where = rows_of(offset, other, chunk)
        return pltpu.make_async_remote_copy(
            src_ref=blocks.at[where], dst_ref=blocks.at[where],
            send_sem=twin_send.at[index], recv_sem=twin_recv.at[index],
            device_id=(twin, me_z), device_id_type=MESH,
        )

    flying = {}
    for turn in range(per_block):
        if turn >= 1 and 2 * turn < per_block:
            masked(order[2 * turn])
            masked(order[2 * turn + 1])
        if turn < min(WINDOW, rounds):
            flying[turn] = [started(ring(way, turn, False)) for way in (0, 1)]
    for chunk in range(per_block):
        go(to_twin(0, False, chunk, chunk))

    depth = BLK * 4 if aux % (BLK * 4) == 0 else BLK

    @pl.loop(0, aux // depth)
    def _(k):
        at_k = pl.ds(pl.multiple_of(k * depth, depth), depth)
        own_t[at_k, :] = blocks[own_rows, at_k].astype(jnp.float32).T.astype(jnp.bfloat16)

    turned[...] = jnp.broadcast_to(virt_energy[...], (virt, virt)).T

    @pl.loop(0, groups * occ_g)
    def _(j):
        for part in range(per_orbital):
            for q in range(shards):
                low = part * PIECE + q * share
                energy[j * per_orbital + part, q] = turned[low:low + share, :] - occ_energy[j]

    own_energy = jnp.concatenate([virt_energy[...] - occ_energy[me_g * occ_g + i] for i in range(occ_g)], axis=1)

    def product(batch, number):
        part32[...] = jnp.zeros_like(part32)

        @pl.loop(0, aux // depth)
        def _(k):
            at_k = pl.ds(pl.multiple_of(k * depth, depth), depth)
            left_side = jnp.concatenate([blocks[rows_of(*entry), at_k] for entry in batch], axis=0)
            part32[...] += jnp.dot(left_side, own_t[at_k, :], preferred_element_type=jnp.float32)

        for c in range(len(batch)):
            for q in range(shards):
                low = c * PIECE + q * share
                part16[number, q, c] = part32[low:low + share, :].astype(jnp.bfloat16)
        for q, z in enumerate(peers):
            go(pltpu.make_async_remote_copy(
                src_ref=part16.at[number, z], dst_ref=arrived.at[number, q],
                send_sem=part_send.at[number, q], recv_sem=part_recv.at[number, q],
                device_id=(me_g, z), device_id_type=MESH,
            ))

    def divide(batch, number):
        for q in range(shards - 1):
            pltpu.make_async_copy(arrived.at[number, q], arrived.at[number, q], part_recv.at[number, q]).wait()
        for c, (offset, other, chunk) in enumerate(batch):
            total = part16[number, me_z, c].astype(jnp.float32)
            for q in range(shards - 1):
                total += arrived[number, q, c].astype(jnp.float32)
            theirs = energy[per_block * at(offset, other) + chunk, me_z]
            gap = jnp.concatenate([theirs] * occ_g, axis=1) + own_energy
            amp[number, me_z, c] = (total / gap).astype(jnp.bfloat16)
        for q, z in enumerate(peers):
            go(pltpu.make_async_remote_copy(
                src_ref=amp.at[number, me_z], dst_ref=amp.at[number, me_z],
                send_sem=amp_send.at[number, q], recv_sem=amp_recv.at[number, q],
                device_id=(me_g, z), device_id_type=MESH,
            ))

    seen = {}

    def combine(batch, number):
        for q, z in enumerate(before):
            slot = amp.at[number, z]
            pltpu.make_async_copy(slot, slot, amp_recv.at[number, q]).wait()
        for c, (offset, other, chunk) in enumerate(batch):
            j = chunk // per_orbital
            key = (offset % chips, other, j)
            seen.setdefault(key, {})[chunk % per_orbital] = (number, c)
            if len(seen[key]) < per_orbital:
                continue
            for part, (n, at_c) in seen[key].items():
                for q in range(shards):
                    low = part * PIECE + q * share
                    tile32[low:low + share, :] = amp[n, q, at_c].astype(jnp.float32)
            columns = pl.ds(pl.multiple_of(at(offset, other) * rows + j * virt, virt), virt)
            for i in range(occ_g):
                tile = tile32[:, i * virt:(i + 1) * virt]
                weight[i * virt:(i + 1) * virt, columns] = (2.0 * tile.T - tile).astype(jnp.bfloat16)

    home = [(0, False, c) for c in range(per_block)] + [(0, True, c) for c in range(per_block)]
    batches = [home[b:b + 4] for b in range(0, len(home), 4)]
    first = len(batches)
    for number, batch in enumerate(batches):
        for offset, other, chunk in batch:
            if other:
                to_twin(0, True, chunk, chunk).wait_recv()
        product(batch, number)
        if number >= 1:
            divide(batches[number - 1], number - 1)
        if number >= 2:
            combine(batches[number - 2], number - 2)
    for turn in range(rounds):
        number = first + turn
        batch = []
        for way in (0, 1):
            step, chunk = place_of(way, turn)
            batch.append((-step if way == 0 else step, False, chunk))
        for way in (0, 1):
            ring(way, turn, True).wait_recv()
            go(to_twin(*batch[way], per_block + 2 * turn + way))
        for copy in flying[turn]:
            copy.wait_send()
        if turn + WINDOW < rounds:
            flying[turn + WINDOW] = [started(ring(way, turn + WINDOW, False)) for way in (0, 1)]
        for way in (0, 1):
            offset, _, chunk = batch[way]
            to_twin(offset, True, chunk, per_block + 2 * turn + way).wait_recv()
        batch = batch + [(offset, True, chunk) for offset, _, chunk in batch]
        batches.append(batch)
        product(batch, number)
        divide(batches[number - 1], number - 1)
        if number >= 2:
            combine(batches[number - 2], number - 2)
    last = len(batches) - 1
    combine(batches[last - 1], last - 1)
    divide(batches[last], last)
    combine(batches[last], last)

    wide = depth
    turns = aux // wide

    def out_copy(c, q, z, source):
        return pltpu.make_async_remote_copy(
            src_ref=staged.at[z, :, :, pl.ds(pl.multiple_of(c * wide, wide), wide)],
            dst_ref=out.at[:, :, pl.ds(pl.multiple_of(source * aux + c * wide, wide), wide)],
            send_sem=out_send.at[c, q], recv_sem=out_recv.at[c, q],
            device_id=(me_g, z), device_id_type=MESH,
        )

    def out_own(c):
        return pltpu.make_async_copy(
            staged.at[me_z, :, :, pl.ds(pl.multiple_of(c * wide, wide), wide)],
            out.at[:, :, pl.ds(pl.multiple_of(me_z * aux + c * wide, wide), wide)],
            out_local.at[c],
        )

    @pl.loop(0, turns)
    def _(c):
        here = pl.ds(pl.multiple_of(c * wide, wide), wide)
        gamma = jnp.dot(weight[...], blocks[:, here], preferred_element_type=jnp.float32)
        for i in range(occ_g):
            for q in range(shards):
                low = i * virt + q * slab
                staged[q, i, :, here] = gamma[low:low + slab, :].astype(jnp.bfloat16)
        for q, z in enumerate(peers):
            out_copy(c, q, z, me_z).start()
        out_own(c).start()

    for copy in sent:
        copy.wait_send()

    @pl.loop(0, turns)
    def _(c):
        for q, z in enumerate(peers):
            out_copy(c, q, z, me_z).wait_send()
            out_copy(c, q, z, before[q]).wait_recv()
        out_own(c).wait()


def on_device(factors, screen, occ_energy, virt_energy):
    occ_g, virt, aux = factors.shape
    groups, shards = lax.axis_size("grp"), lax.axis_size("sh")
    rows = occ_g * virt
    per_block = rows // PIECE
    share = PIECE // shards
    slab = virt // shards
    span = groups // 4
    rounds = per_block * (span - 1) + per_block // 2
    batches = groups * per_block // 4
    turns = aux // (BLK * 4 if aux % (BLK * 4) == 0 else BLK)
    dma = pltpu.SemaphoreType.DMA
    bf16 = jnp.bfloat16
    smem = pl.BlockSpec(memory_space=pltpu.SMEM)
    return pl.pallas_call(
        functools.partial(amplitude_kernel, (occ_g, virt, aux, groups, shards)),
        out_shape=jax.ShapeDtypeStruct((occ_g, slab, aux * shards), bf16),
        in_specs=[pl.BlockSpec(memory_space=pl.ANY), smem, smem, pl.BlockSpec(memory_space=pltpu.VMEM)],
        out_specs=pl.BlockSpec(memory_space=pl.ANY),
        scratch_shapes=[
            pltpu.VMEM((groups * rows, aux), bf16),
            pltpu.VMEM((aux, rows), bf16),
            pltpu.VMEM((4 * PIECE, rows), jnp.float32),
            pltpu.VMEM((batches, shards, 4, share, rows), bf16),
            pltpu.VMEM((batches, shards - 1, 4, share, rows), bf16),
            pltpu.VMEM((batches, shards, 4, share, rows), bf16),
            pltpu.VMEM((virt, rows), jnp.float32),
            pltpu.VMEM((virt, virt), jnp.float32),
            pltpu.VMEM((groups * per_block, shards, share, virt), jnp.float32),
            pltpu.VMEM((rows, groups * rows), bf16),
            pltpu.VMEM((shards, occ_g, slab, aux), bf16),
            dma((per_block,)),
            dma((2, rounds)),
            dma((2, rounds)),
            dma((groups * per_block // 2,)),
            dma((groups * per_block // 2,)),
            dma((batches, shards - 1)),
            dma((batches, shards - 1)),
            dma((batches, shards - 1)),
            dma((batches, shards - 1)),
            dma((turns, shards - 1)),
            dma((turns, shards - 1)),
            dma((turns,)),
        ],
        cost_estimate=pl.CostEstimate(
            flops=4 * rows * groups * rows * aux, bytes_accessed=4 * rows * aux, transcendentals=0
        ),
        compiler_params=pltpu.CompilerParams(
            collective_id=0, has_side_effects=True, vmem_limit_bytes=56 * 1024 * 1024
        ),
    )(factors.reshape(rows, aux), screen, occ_energy, virt_energy.reshape(1, virt))


def solution(mesh):
    placed = (P("grp", None, "sh"), P("grp", None, "sh"), P(), P())
    return jax.shard_map(
        on_device, mesh=mesh, in_specs=placed, out_specs=P("grp", "sh", None), check_vma=False
    )
```
